256 devices in a mesh: dp: 64 (over z, x_lo, y), tensor: 4 (over x_hi, core).
Axes of the slice: x: 4 (x_hi: 2, x_lo: 2; x = x_hi * 2 + x_lo), y: 4, z: 8, core: 2. Of those that a mesh axis runs over, the one named last changes fastest.
Arguments:
- activations: bfloat16 [2, 24576, 4096], P(None, 'dp', 'tensor'), may hold values from -6 to 6
- signals: bfloat16 [3, 24576, 11008], P(None, 'dp', 'tensor'), may hold values from -6 to 6
- projectors: bfloat16 [3, 4096, 128], replicated, may hold values from -0.09375 to 0.09375
- weights: bfloat16 [3, 4096, 11008], P(None, 'dp', 'tensor'), may hold values from -0.09375 to 0.09375
- first_moment: float32 [3, 128, 11008], P(None, 'dp', 'tensor'), may hold values from -0.02734375 to 0.02734375
- second_moment: float32 [3, 128, 11008], P(None, 'dp', 'tensor'), may hold values from 8.138021e-06 to 0.00016276042
Outputs:
- new_weights: bfloat16 [3, 4096, 11008], P(None, 'dp', 'tensor')
- new_first: float32 [3, 128, 11008], P(None, 'dp', 'tensor')
- new_second: float32 [3, 128, 11008], P(None, 'dp', 'tensor')
- direction: float32 [3, 128, 11008], P(None, 'dp', 'tensor')
The draws below stay inside these ranges and needn't reach their ends.
All inputs are finite; a program needn't handle non-finite values.
Results may differ from the reference program's by a relative error of at most 0.0044.
Values may be sent and summed in bfloat16 or wider, within the bound.
A program may use at most 64 MiB of HBM per device.

```python
import math
import jax
import jax.numpy as jnp
from jax import lax

D = 4096
FF = 11008
R = 128
TOKENS = 24576


def levels(key, extent, pieces, least, high):
    gain, own = 1.0, jax.random.fold_in(key, 6)
    for dim, shards_of in pieces:
        steps = jnp.exp(jax.random.uniform(jax.random.fold_in(own, dim), (shards_of,), jnp.float32, least / len(pieces), high / len(pieces)))
        gain = gain * jnp.repeat(steps, extent[dim] // shards_of).reshape([-1 if axis == dim else 1 for axis in range(len(extent))])
    return gain


def centred(own_key, shape, width, limit, cuts=(), kind=jnp.bfloat16):
    drawn = width * jax.random.normal(own_key, shape, jnp.float32)
    if cuts:
        drawn = drawn * levels(own_key, shape, cuts, -0.22, 0.18)
    return jnp.clip(drawn, -limit, limit).astype(kind)


def setup_inputs(seed: int = 0) -> dict:
    arg_keys = jax.random.split(jax.random.key(seed), 7)
    activations = centred(arg_keys[0], (2, TOKENS, D), 1.0, 6.0, ((1, 64), (2, 4)))
    signals = centred(arg_keys[1], (3, TOKENS, FF), 1.0, 6.0, ((1, 64), (2, 4)))
    projectors = centred(arg_keys[2], (3, D, R), D ** -0.5, 0.09375)
    weights = centred(arg_keys[3], (3, D, FF), D ** -0.5, 0.09375, ((1, 64), (2, 4)))
    first_moment = centred(arg_keys[4], (3, R, FF), (0.3 / TOKENS ** 0.5), 0.02734375, ((1, 64), (2, 4)), jnp.float32)
    second_moment = jnp.clip(jnp.exp(math.log(0.00016276042) - 2.9957323 * jax.random.uniform(arg_keys[5], (3, R, FF), jnp.float32) ** levels(arg_keys[5], (3, R, FF), ((1, 64), (2, 4)), -0.2, 0.2)), 8.138021257764194e-06, 0.00016276042)
    return dict(activations=activations, signals=signals, projectors=projectors, weights=weights, first_moment=first_moment, second_moment=second_moment)


beta_one = 0.9
beta_two = 0.999
adam_step = 1000
adam_eps = 1e-08
learning_rate = 0.05
first_fix = 1.0 - beta_one ** adam_step
second_fix = 1.0 - beta_two ** adam_step

def reference(activations, signals, projectors, weights, first_moment, second_moment):
    sources = (activations[0], activations[0], activations[1])
    out_weights = []
    out_first = []
    out_second = []
    out_heading = []
    for index in range(3):
        proj_acts = jnp.dot(sources[index], projectors[index], preferred_element_type=jnp.float32).astype(jnp.bfloat16)
        gradient = jnp.dot(proj_acts.T, signals[index], preferred_element_type=jnp.float32) / TOKENS
        moment_one = beta_one * first_moment[index] + (1.0 - beta_one) * gradient
        moment_two = beta_two * second_moment[index] + (1.0 - beta_two) * gradient * gradient
        heading = moment_one / first_fix / (jnp.sqrt(moment_two / second_fix) + adam_eps)
        change = jnp.dot(projectors[index].astype(jnp.float32), heading, precision=lax.Precision.HIGHEST)
        updated = (weights[index].astype(jnp.float32) - learning_rate * change).astype(jnp.bfloat16)
        out_weights.append(updated)
        out_first.append(moment_one)
        out_second.append(moment_two)
        out_heading.append(heading)
    return (jnp.stack(out_weights), jnp.stack(out_first), jnp.stack(out_second), jnp.stack(out_heading))
```

```python
import functools

import jax
import jax.numpy as jnp
from jax import lax
from jax.experimental import pallas as pl
from jax.experimental.pallas import tpu as pltpu
from jax.sharding import PartitionSpec as P

MESH = pl.DeviceIdType.MESH
F32, BF16 = jnp.float32, jnp.bfloat16

beta_one = 0.9
beta_two = 0.999
adam_step = 1000
adam_eps = 1e-08
learning_rate = 0.05
first_fix = 1.0 - beta_one**adam_step
second_fix = 1.0 - beta_two**adam_step

NZ, NX, NY = 8, 2, 4
SIZES = {"z": NZ, "y": NY, "x": NX, "xy": NX * NY}
ROUTES = (("z", "xy"), ("y", "x", "z"), ("x", "y", "z"))
BLOCK = 512


def blocks(width):
    return [(at, min(BLOCK, width - at)) for at in range(0, width, BLOCK)]


def route_rows(route):
    return tuple(SIZES[g] for g in route[:-1])


def permutation(route, count):
    p = lax.broadcasted_iota(jnp.int32, (count, count), 0)
    r = lax.broadcasted_iota(jnp.int32, (count, count), 1)
    parts, rest = {}, p // 2
    for g in reversed(route):
        parts[g] = rest % SIZES[g]
        rest = rest // SIZES[g]
    if "xy" in parts:
        parts["x"], parts["y"] = parts["xy"] // NY, parts["xy"] % NY
    natural = ((parts["z"] * NX + parts["x"]) * NY + parts["y"]) * 2 + p % 2
    return (natural == r).astype(F32).astype(BF16)


def kernel(
    act, sig, proj, weights, first, second,
    new_weights, new_first, new_second, new_dir,
    act_v, sig_v, p_v, ploc_v, w_v, m1_v, m2_v, o1_v, o2_v, od_v, wo_v,
    qp, rc, sx, rx, q_v,
    g0, g1, g2, r10, r11, r12, s21, s22, r21, r22, sl, rl, gl, d0, d1, d2,
    lsem, ssem, rsem,
):
    dp, tp = lax.axis_index("dp"), lax.axis_index("tensor")
    z, xl, y = dp // (NX * NY), (dp // NY) % NX, dp % NY
    xh, core = tp // 2, tp % 2
    tokens, depth = act_v.shape[1], act_v.shape[2]
    width = sig_v.shape[1]
    half = tokens // 2
    rows = w_v.shape[1]

    def device(zz, xx, yy, hh=None, cc=None):
        hh = xh if hh is None else hh
        cc = core if cc is None else cc
        return ((zz * NX + xx) * NY + yy, hh * 2 + cc)

    index = {"z": z, "y": y, "x": xl, "xy": xl * NY + y}

    def peer(group, d):
        if group == "z":
            to, frm = (z + d) % NZ, (z + NZ - d) % NZ
            return device(to, xl, y), to, frm
        if group == "y":
            to, frm = (y + d) % NY, (y + NY - d) % NY
            return device(z, xl, to), to, frm
        if group == "x":
            return device(z, 1 - xl, y), 1 - xl, 1 - xl
        dx, dy = d // NY, d % NY
        xx = 1 - xl if dx else xl
        to, frm = (y + dy) % NY, (y + NY - dy) % NY
        return device(z, xx, to), xx * NY + to, xx * NY + frm

    core_peer = device(z, xl, y, xh, 1 - core)
    high_peer = device(z, xl, y, 1 - xh, core)

    loads = {}

    def load(name, src, dst):
        c = pltpu.make_async_copy(src, dst, lsem.at[len(loads)])
        c.start()
        loads[name] = c

    part = pl.ds(pl.multiple_of(tp * depth, depth), depth)
    load("a0", act.at[0], act_v.at[0])
    load("p0", proj.at[0, part], p_v.at[0])
    load("p1", proj.at[1, part], p_v.at[1])
    load("a1", act.at[1], act_v.at[1])
    load("p2", proj.at[2, part], p_v.at[2])
    for k in range(3):
        load(f"s{k}", sig.at[k], sig_v.at[k])
    own = pl.ds(pl.multiple_of(dp * rows, rows), rows)
    load("pl", proj.at[:, own], ploc_v)
    load("m1", first, m1_v)
    load("m2", second, m2_v)
    load("w", weights, w_v)

    barrier = pltpu.get_barrier_semaphore()
    partners = [core_peer, high_peer]
    partners += [peer("z", d)[0] for d in range(1, NZ)]
    partners += [peer("xy", d)[0] for d in range(1, NX * NY)]
    for p in partners:
        pl.semaphore_signal(barrier, inc=1, device_id=p, device_id_type=MESH)

    sends = []

    def remote(src, dst, sem, to):
        return pltpu.make_async_remote_copy(
            src_ref=src, dst_ref=dst, send_sem=ssem.at[sem], recv_sem=rsem.at[sem],
            device_id=to, device_id_type=MESH,
        )

    def send(src, dst, sem, to):
        c = remote(src, dst, sem, to)
        c.start()
        sends.append(c)

    counter = [0]

    def sems(n):
        counter[0] += n
        return counter[0] - n

    core_one, high_one, core_two = sems(3), sems(3), sems(3)

    def project(k):
        source = (0, 0, 1)[k]
        value = jnp.dot(act_v[source], p_v[k], preferred_element_type=F32)
        qp[k] = value.reshape(2, half, value.shape[1])

    for k in range(3):
        if k != 1:
            loads[("a0", "", "a1")[k]].wait()
        loads[f"p{k}"].wait()
        project(k)
        if k == 0:
            pl.semaphore_wait(barrier, len(partners))
        send(qp.at[k, 1 - core], rc.at[k], core_one + k, core_peer)
    for k in range(3):
        remote(qp.at[k, 0], rc.at[k], core_one + k, core_peer).wait_recv()
        total = qp[k, core] + rc[k]
        rc[k] = total
        sx[k] = total.astype(BF16)
        send(sx.at[k], rx.at[k], high_one + k, high_peer)
    for k in range(3):
        remote(sx.at[k], rx.at[k], high_one + k, high_peer).wait_recv()
        q_v[k, core] = (rc[k] + rx[k].astype(F32)).astype(BF16)
        send(q_v.at[k, core], q_v.at[k, core], core_two + k, core_peer)

    grads = (g0, g1, g2)
    firsts = (r10, r11, r12)
    seconds = (None, s21, s22)
    second_recv = (None, r21, r22)
    dirs = (d0, d1, d2)
    perms = [permutation(route, 128) for route in ROUTES]
    base = [[sems(SIZES[g] - 1) for g in route] for route in ROUTES]
    base_back = [[sems(SIZES[g] - 1) for g in route] for route in ROUTES]

    def scatter(k, stage, src, recv):
        group = ROUTES[k][stage]
        for d in range(1, SIZES[group]):
            to, idx, _ = peer(group, d)
            send(src.at[idx], recv.at[d - 1], base[k][stage] + d - 1, to)

    def arrived(k, stage, src, recv):
        group = ROUTES[k][stage]
        for d in range(1, SIZES[group]):
            to, idx, _ = peer(group, d)
            remote(src.at[idx], recv.at[d - 1], base[k][stage] + d - 1, to).wait_recv()

    for k in range(3):
        route = ROUTES[k]
        remote(q_v.at[k, 1 - core], q_v.at[k, 1 - core], core_two + k, core_peer).wait_recv()
        q = q_v[k].reshape(tokens, 128)
        turned = lax.dot_general(
            perms[k], q, (((1,), (1,)), ((), ())), preferred_element_type=F32
        ).astype(BF16)
        loads[f"s{k}"].wait()
        lead = grads[k].shape[:-1]
        for at, w in blocks(width):
            value = lax.dot_general(
                turned, sig_v[k, at : at + w, :], (((1,), (1,)), ((), ())), preferred_element_type=F32
            )
            grads[k][..., at : at + w] = value.astype(BF16).reshape(lead + (w,))
        scatter(k, 0, grads[k], firsts[k])

    def summed(src, recv, idx, at, w):
        total = src[idx, ..., at : at + w].astype(F32)
        for i in range(recv.shape[0]):
            total = total + recv[i, ..., at : at + w].astype(F32)
        return total

    def to_pieces(k, total, at, w):
        for i in range(8):
            sl[k, i, :, at : at + w] = total[2 * i : 2 * i + 2].astype(BF16)

    def first_sum(k):
        route = ROUTES[k]
        arrived(k, 0, grads[k], firsts[k])
        for at, w in blocks(width):
            total = summed(grads[k], firsts[k], index[route[0]], at, w)
            if len(route) == 2:
                to_pieces(k, total, at, w)
            else:
                seconds[k][:, :, at : at + w] = total.astype(BF16)
        if len(route) == 2:
            scatter(k, 1, sl.at[k], rl.at[k])
        else:
            scatter(k, 1, seconds[k], second_recv[k])

    def second_sum(k):
        route = ROUTES[k]
        arrived(k, 1, seconds[k], second_recv[k])
        for at, w in blocks(width):
            to_pieces(k, summed(seconds[k], second_recv[k], index[route[1]], at, w), at, w)
        scatter(k, 2, sl.at[k], rl.at[k])

    outs = []
    count = float(tokens * NZ * NX * NY)

    def store(src, dst):
        c = pltpu.make_async_copy(src, dst, lsem.at[len(loads) + len(outs)])
        c.start()
        outs.append(c)

    def update(k):
        route = ROUTES[k]
        last = len(route) - 1
        arrived(k, last, sl.at[k], rl.at[k])
        idx = index[route[last]]
        for at, w in blocks(width):
            cols = slice(at, at + w)
            gradient = summed(sl.at[k], rl.at[k], idx, at, w) / count
            one = beta_one * m1_v[k, :, cols] + (1.0 - beta_one) * gradient
            two = beta_two * m2_v[k, :, cols] + (1.0 - beta_two) * gradient * gradient
            heading = one / first_fix / (jnp.sqrt(two / second_fix) + adam_eps)
            o1_v[k, :, cols] = one
            o2_v[k, :, cols] = two
            od_v[k, :, cols] = heading
            gl[k, idx, :, cols] = heading.astype(BF16)
        for d in range(1, SIZES[route[last]]):
            to, _, _ = peer(route[last], d)
            send(gl.at[k, idx], gl.at[k, idx], base_back[k][last] + d - 1, to)

    def place(k, stage):
        return tuple(index[g] for g in ROUTES[k][: stage + 1])

    def spread(k, stage):
        group = ROUTES[k][stage]
        at = place(k, stage)
        for d in range(1, SIZES[group]):
            to, _, _ = peer(group, d)
            send(dirs[k].at[at], dirs[k].at[at], base_back[k][stage] + d - 1, to)

    def gathered(k, stage):
        group = ROUTES[k][stage]
        lead = place(k, stage)[:-1]
        for d in range(1, SIZES[group]):
            to, _, frm = peer(group, d)
            slot = dirs[k].at[lead + (frm,)]
            remote(slot, slot, base_back[k][stage] + d - 1, to).wait_recv()

    def joined(k):
        route = ROUTES[k]
        last = len(route) - 1
        for d in range(1, SIZES[route[last]]):
            to, _, frm = peer(route[last], d)
            remote(gl.at[k, frm], gl.at[k, frm], base_back[k][last] + d - 1, to).wait_recv()
        at16 = place(k, last - 1)
        for at, w in blocks(width):
            pieces = [gl[k, i, :, at : at + w].astype(F32) for i in range(8)]
            dirs[k][at16 + (slice(None), slice(at, at + w))] = jnp.concatenate(pieces, axis=0).astype(BF16)
        spread(k, last - 1)

    def finish(k):
        gathered(k, 0)
        basis = lax.dot_general(
            ploc_v[k], perms[k], (((1,), (1,)), ((), ())), preferred_element_type=F32
        ).astype(BF16)
        for at, w in blocks(width):
            cols = slice(at, at + w)
            heading = dirs[k][..., cols].reshape(128, w)
            change = jnp.dot(basis, heading, preferred_element_type=F32)
            wo_v[k, :, cols] = (w_v[k, :, cols].astype(F32) - learning_rate * change).astype(BF16)
        store(wo_v.at[k], new_weights.at[k])

    first_sum(1)
    first_sum(2)
    second_sum(1)
    loads["m1"].wait()
    loads["m2"].wait()
    second_sum(2)
    update(1)
    update(2)
    first_sum(0)
    joined(1)
    joined(2)
    update(0)
    store(o1_v, new_first)
    store(o2_v, new_second)
    store(od_v, new_dir)
    gathered(1, 1)
    spread(1, 0)
    gathered(2, 1)
    spread(2, 0)
    joined(0)
    loads["pl"].wait()
    loads["w"].wait()
    finish(1)
    finish(2)
    finish(0)
    for c in sends:
        c.wait_send()
    for c in outs:
        c.wait()


def on_device(activations, signals, projectors, weights, first_moment, second_moment):
    signals = jnp.transpose(signals, (0, 2, 1))
    _, tokens, depth = activations.shape
    _, width, _ = signals.shape
    rank = projectors.shape[2]
    rows = weights.shape[1]
    half = tokens // 2
    small = first_moment.shape
    vmem = pltpu.VMEM
    lead = [route_rows(r) for r in ROUTES]
    cell = (16, width)

    scratch = [
        vmem(activations.shape, BF16), vmem(signals.shape, BF16), vmem((3, depth, rank), BF16),
        vmem((3, rows, rank), BF16), vmem(weights.shape, BF16), vmem(small, F32), vmem(small, F32),
        vmem(small, F32), vmem(small, F32), vmem(small, F32), vmem(weights.shape, BF16),
        vmem((3, 2, half, rank), F32), vmem((3, half, rank), F32), vmem((3, half, rank), BF16),
        vmem((3, half, rank), BF16), vmem((3, 2, half, rank), BF16),
    ]
    scratch += [vmem(l + cell, BF16) for l in lead]
    scratch += [vmem((l[0] - 1,) + l[1:] + cell, BF16) for l in lead]
    scratch += [vmem(l[1:] + cell, BF16) for l in lead[1:]]
    scratch += [vmem((l[1] - 1,) + cell, BF16) for l in lead[1:]]
    scratch += [
        vmem((3, 8, 2, width), BF16), vmem((3, 7, 2, width), BF16), vmem((3, 8, 2, width), BF16),
    ]
    scratch += [vmem(l + cell, BF16) for l in lead]
    scratch += [
        pltpu.SemaphoreType.DMA((24,)), pltpu.SemaphoreType.DMA((96,)), pltpu.SemaphoreType.DMA((96,)),
    ]
    return pl.pallas_call(
        kernel,
        out_shape=(
            jax.ShapeDtypeStruct(weights.shape, BF16),
            jax.ShapeDtypeStruct(small, F32),
            jax.ShapeDtypeStruct(small, F32),
            jax.ShapeDtypeStruct(small, F32),
        ),
        in_specs=[pl.BlockSpec(memory_space=pl.ANY)] * 6,
        out_specs=(pl.BlockSpec(memory_space=pl.ANY),) * 4,
        scratch_shapes=scratch,
        compiler_params=pltpu.CompilerParams(
            collective_id=0, has_side_effects=True, vmem_limit_bytes=48 << 20
        ),
        name="lowrank_adam",
    )(activations, signals, projectors, weights, first_moment, second_moment)


def solution(mesh):
    split = P(None, "dp", "tensor")
    return jax.shard_map(
        on_device,
        mesh=mesh,
        in_specs=(split, split, P(), split, split, split),
        out_specs=(split, split, split, split),
        check_vma=False,
    )
```

```python
import functools

import jax
import jax.numpy as jnp
from jax import lax
from jax.experimental import pallas as pl
from jax.experimental.pallas import tpu as pltpu
from jax.sharding import PartitionSpec as P

MESH = pl.DeviceIdType.MESH
F32, BF16 = jnp.float32, jnp.bfloat16

beta_one = 0.9
beta_two = 0.999
adam_step = 1000
adam_eps = 1e-08
learning_rate = 0.05
first_fix = 1.0 - beta_one**adam_step
second_fix = 1.0 - beta_two**adam_step

NZ, NX, NY = 8, 2, 4
SIZES = {"z": NZ, "y": NY, "x": NX, "xy": NX * NY}
AROUND, ACROSS, ALONG = ("z", "xy"), ("y", "x", "z"), ("x", "y", "z")
CUT = 1408
PARTS = (
    (0, 0, ALONG), (0, 1, ACROSS), (1, 0, ALONG), (1, 1, AROUND), (2, 0, ALONG), (2, 1, ACROSS),
)
BLOCK = 512


def span(part, width):
    return (0, CUT) if part[1] == 0 else (CUT, width - CUT)


def blocks(width):
    return [(at, min(BLOCK, width - at)) for at in range(0, width, BLOCK)]


def route_rows(route):
    return tuple(SIZES[g] for g in route[:-1])


def permutation(route, count):
    p = lax.broadcasted_iota(jnp.int32, (count, count), 0)
    r = lax.broadcasted_iota(jnp.int32, (count, count), 1)
    parts, rest = {}, p // 2
    for g in reversed(route):
        parts[g] = rest % SIZES[g]
        rest = rest // SIZES[g]
    if "xy" in parts:
        parts["x"], parts["y"] = parts["xy"] // NY, parts["xy"] % NY
    natural = ((parts["z"] * NX + parts["x"]) * NY + parts["y"]) * 2 + p % 2
    return (natural == r).astype(F32).astype(BF16)


def kernel(
    act, sig, proj, weights, first, second,
    new_weights, new_first, new_second, new_dir,
    act_v, sig_v, p_v, ploc_v, w_v, m1_v, m2_v, qp, rc, sx, rx, q_v, *rest,
):
    n = len(PARTS)
    grads, firsts, seconds, second_recv, sl, rl, gl, dirs = (rest[i * n : (i + 1) * n] for i in range(8))
    lsem, ssem, rsem = rest[8 * n :]
    dp, tp = lax.axis_index("dp"), lax.axis_index("tensor")
    z, xl, y = dp // (NX * NY), (dp // NY) % NX, dp % NY
    xh, core = tp // 2, tp % 2
    tokens, depth = act_v.shape[1], act_v.shape[2]
    width = sig_v.shape[1]
    half = tokens // 2
    rows = w_v.shape[1]

    def device(zz, xx, yy, hh=None, cc=None):
        hh = xh if hh is None else hh
        cc = core if cc is None else cc
        return ((zz * NX + xx) * NY + yy, hh * 2 + cc)

    index = {"z": z, "y": y, "x": xl, "xy": xl * NY + y}

    def peer(group, d):
        if group == "z":
            to, frm = (z + d) % NZ, (z + NZ - d) % NZ
            return device(to, xl, y), to, frm
        if group == "y":
            to, frm = (y + d) % NY, (y + NY - d) % NY
            return device(z, xl, to), to, frm
        if group == "x":
            return device(z, 1 - xl, y), 1 - xl, 1 - xl
        dx, dy = d // NY, d % NY
        xx = 1 - xl if dx else xl
        to, frm = (y + dy) % NY, (y + NY - dy) % NY
        return device(z, xx, to), xx * NY + to, xx * NY + frm

    core_peer = device(z, xl, y, xh, 1 - core)
    high_peer = device(z, xl, y, 1 - xh, core)

    loads = {}

    def load(name, src, dst):
        c = pltpu.make_async_copy(src, dst, lsem.at[len(loads)])
        c.start()
        loads[name] = c

    part = pl.ds(pl.multiple_of(tp * depth, depth), depth)
    load("a0", act.at[0], act_v.at[0])
    load("p0", proj.at[0, part], p_v.at[0])
    load("p1", proj.at[1, part], p_v.at[1])
    load("a1", act.at[1], act_v.at[1])
    load("p2", proj.at[2, part], p_v.at[2])
    for k in range(3):
        load(f"s{k}", sig.at[k], sig_v.at[k])
    own = pl.ds(pl.multiple_of(dp * rows, rows), rows)
    load("pl", proj.at[:, own], ploc_v)
    load("m1", first, m1_v)
    load("m2", second, m2_v)
    load("w", weights, w_v)

    barrier = pltpu.get_barrier_semaphore()
    partners = [core_peer, high_peer]
    partners += [peer("z", d)[0] for d in range(1, NZ)]
    partners += [peer("xy", d)[0] for d in range(1, NX * NY)]
    for p in partners:
        pl.semaphore_signal(barrier, inc=1, device_id=p, device_id_type=MESH)

    sends = []

    def remote(src, dst, sem, to):
        return pltpu.make_async_remote_copy(
            src_ref=src, dst_ref=dst, send_sem=ssem.at[sem], recv_sem=rsem.at[sem],
            device_id=to, device_id_type=MESH,
        )

    def send(src, dst, sem, to):
        c = remote(src, dst, sem, to)
        c.start()
        sends.append(c)

    counter = [0]

    def sems(n):
        counter[0] += n
        return counter[0] - n

    core_one, high_one, core_two = sems(3), sems(3), sems(3)

    def project(k):
        source = (0, 0, 1)[k]
        value = jnp.dot(act_v[source], p_v[k], preferred_element_type=F32)
        qp[k] = value.reshape(2, half, value.shape[1])

    perms = {route: permutation(route, 128) for route in {p[2]: 0 for p in PARTS}}
    base = [[sems(SIZES[g] - 1) for g in p[2]] for p in PARTS]
    base_back = [[sems(SIZES[g] - 1) for g in p[2]] for p in PARTS]

    def core_send(k):
        if k != 1:
            loads[("a0", "", "a1")[k]].wait()
        loads[f"p{k}"].wait()
        project(k)
        if k == 0:
            pl.semaphore_wait(barrier, len(partners))
        send(qp.at[k, 1 - core], rc.at[k], core_one + k, core_peer)

    def high_send(k):
        remote(qp.at[k, 0], rc.at[k], core_one + k, core_peer).wait_recv()
        total = qp[k, core] + rc[k]
        rc[k] = total
        sx[k] = total.astype(BF16)
        send(sx.at[k], rx.at[k], high_one + k, high_peer)

    def core_back(k):
        remote(sx.at[k], rx.at[k], high_one + k, high_peer).wait_recv()
        q_v[k, core] = (rc[k] + rx[k].astype(F32)).astype(BF16)
        send(q_v.at[k, core], q_v.at[k, core], core_two + k, core_peer)

    def scatter(p, stage, src, recv):
        group = PARTS[p][2][stage]
        for d in range(1, SIZES[group]):
            to, idx, _ = peer(group, d)
            send(src.at[idx], recv.at[d - 1], base[p][stage] + d - 1, to)

    def arrived(p, stage, src, recv):
        group = PARTS[p][2][stage]
        for d in range(1, SIZES[group]):
            to, idx, _ = peer(group, d)
            remote(src.at[idx], recv.at[d - 1], base[p][stage] + d - 1, to).wait_recv()

    def gradient_of(k):
        remote(q_v.at[k, 1 - core], q_v.at[k, 1 - core], core_two + k, core_peer).wait_recv()
        q = q_v[k].reshape(tokens, 128)
        loads[f"s{k}"].wait()
        for p, part in enumerate(PARTS):
            if part[0] != k:
                continue
            turned = lax.dot_general(
                perms[part[2]], q, (((1,), (1,)), ((), ())), preferred_element_type=F32
            ).astype(BF16)
            start, size = span(part, width)
            lead = grads[p].shape[:-1]
            for at, w in blocks(size):
                value = lax.dot_general(
                    turned, sig_v[k, start + at : start + at + w, :], (((1,), (1,)), ((), ())),
                    preferred_element_type=F32,
                )
                grads[p][..., at : at + w] = value.astype(BF16).reshape(lead + (w,))
            scatter(p, 0, grads[p], firsts[p])

    def summed(src, recv, idx, at, w):
        total = src[idx, ..., at : at + w].astype(F32)
        for i in range(recv.shape[0]):
            total = total + recv[i, ..., at : at + w].astype(F32)
        return total

    def to_pieces(p, total, at, w):
        for i in range(8):
            sl[p][i, :, at : at + w] = total[2 * i : 2 * i + 2].astype(BF16)

    def first_sum(p):
        route = PARTS[p][2]
        arrived(p, 0, grads[p], firsts[p])
        for at, w in blocks(span(PARTS[p], width)[1]):
            total = summed(grads[p], firsts[p], index[route[0]], at, w)
            if len(route) == 2:
                to_pieces(p, total, at, w)
            else:
                seconds[p][:, :, at : at + w] = total.astype(BF16)
        if len(route) == 2:
            scatter(p, 1, sl[p], rl[p])
        else:
            scatter(p, 1, seconds[p], second_recv[p])

    def second_sum(p):
        route = PARTS[p][2]
        if len(route) == 2:
            return
        arrived(p, 1, seconds[p], second_recv[p])
        for at, w in blocks(span(PARTS[p], width)[1]):
            to_pieces(p, summed(seconds[p], second_recv[p], index[route[1]], at, w), at, w)
        scatter(p, 2, sl[p], rl[p])

    count = float(tokens * NZ * NX * NY)

    def update(p):
        k, _, route = PARTS[p]
        last = len(route) - 1
        arrived(p, last, sl[p], rl[p])
        idx = index[route[last]]
        start, size = span(PARTS[p], width)
        for at, w in blocks(size):
            cols = slice(start + at, start + at + w)
            gradient = summed(sl[p], rl[p], idx, at, w) / count
            one = beta_one * m1_v[k, :, cols] + (1.0 - beta_one) * gradient
            two = beta_two * m2_v[k, :, cols] + (1.0 - beta_two) * gradient * gradient
            heading = one / first_fix / (jnp.sqrt(two / second_fix) + adam_eps)
            new_first[k, :, cols] = one
            new_second[k, :, cols] = two
            new_dir[k, :, cols] = heading
            gl[p][idx, :, at : at + w] = heading.astype(BF16)
        for d in range(1, SIZES[route[last]]):
            to, _, _ = peer(route[last], d)
            send(gl[p].at[idx], gl[p].at[idx], base_back[p][last] + d - 1, to)

    def place(p, stage):
        return tuple(index[g] for g in PARTS[p][2][: stage + 1])

    def spread(p, stage):
        group = PARTS[p][2][stage]
        at = place(p, stage)
        for d in range(1, SIZES[group]):
            to, _, _ = peer(group, d)
            send(dirs[p].at[at], dirs[p].at[at], base_back[p][stage] + d - 1, to)

    def gathered(p, stage):
        group = PARTS[p][2][stage]
        lead = place(p, stage)[:-1]
        for d in range(1, SIZES[group]):
            to, _, frm = peer(group, d)
            slot = dirs[p].at[lead + (frm,)]
            remote(slot, slot, base_back[p][stage] + d - 1, to).wait_recv()

    def joined(p):
        route = PARTS[p][2]
        last = len(route) - 1
        for d in range(1, SIZES[route[last]]):
            to, _, frm = peer(route[last], d)
            remote(gl[p].at[frm], gl[p].at[frm], base_back[p][last] + d - 1, to).wait_recv()
        at16 = place(p, last - 1)
        for at, w in blocks(span(PARTS[p], width)[1]):
            pieces = [gl[p][i, :, at : at + w].astype(F32) for i in range(8)]
            dirs[p][at16 + (slice(None), slice(at, at + w))] = jnp.concatenate(pieces, axis=0).astype(BF16)
        spread(p, last - 1)

    def middle(p):
        if len(PARTS[p][2]) == 3:
            gathered(p, 1)
            spread(p, 0)

    def finish(p):
        k, _, route = PARTS[p]
        gathered(p, 0)
        basis = lax.dot_general(
            ploc_v[k], perms[route], (((1,), (1,)), ((), ())), preferred_element_type=F32
        ).astype(BF16)
        start, size = span(PARTS[p], width)
        for at, w in blocks(size):
            cols = slice(start + at, start + at + w)
            heading = dirs[p][..., at : at + w].reshape(128, w)
            change = jnp.dot(basis, heading, preferred_element_type=F32)
            new_weights[k, :, cols] = (w_v[k, :, cols].astype(F32) - learning_rate * change).astype(BF16)

    for k in range(3):
        core_send(k)
    for k in range(3):
        high_send(k)
    core_back(0)
    core_back(1)
    gradient_of(0)
    core_back(2)
    gradient_of(1)
    gradient_of(2)

    for name in ("m1", "m2", "pl", "w"):
        loads[name].wait()
    order = (0, 1, 2, 4, 5, 3)
    for p in order:
        first_sum(p)
    for p in order:
        second_sum(p)
    for p in order:
        update(p)
    for p in order:
        joined(p)
    for p in order:
        middle(p)
    for p in order:
        finish(p)
    for c in sends:
        c.wait_send()


def write_out(*refs):
    sem = refs[8]
    copies = [pltpu.make_async_copy(refs[i], refs[4 + i], sem.at[i]) for i in range(4)]
    for c in copies:
        c.start()
    for c in copies:
        c.wait()


def on_device(activations, signals, projectors, weights, first_moment, second_moment):
    signals = jnp.transpose(signals, (0, 2, 1))
    _, tokens, depth = activations.shape
    _, width, _ = signals.shape
    rank = projectors.shape[2]
    rows = weights.shape[1]
    half = tokens // 2
    small = first_moment.shape
    vmem = pltpu.VMEM
    lead = [route_rows(p[2]) for p in PARTS]
    cells = [(16, span(p, width)[1]) for p in PARTS]

    def small_like(n):
        return [vmem((n, 2, c[1]), BF16) for c in cells]

    scratch = [
        vmem(activations.shape, BF16), vmem(signals.shape, BF16), vmem((3, depth, rank), BF16),
        vmem((3, rows, rank), BF16), vmem(weights.shape, BF16), vmem(small, F32), vmem(small, F32),
        vmem((3, 2, half, rank), F32), vmem((3, half, rank), F32), vmem((3, half, rank), BF16),
        vmem((3, half, rank), BF16), vmem((3, 2, half, rank), BF16),
    ]
    scratch += [vmem(l + c, BF16) for l, c in zip(lead, cells)]
    scratch += [vmem((l[0] - 1,) + l[1:] + c, BF16) for l, c in zip(lead, cells)]
    scratch += [vmem((l + (1,))[1:2] + c, BF16) for l, c in zip(lead, cells)]
    scratch += [vmem((max((l + (1,))[1] - 1, 1),) + c, BF16) for l, c in zip(lead, cells)]
    scratch += small_like(8) + small_like(7) + small_like(8)
    scratch += [vmem(l + c, BF16) for l, c in zip(lead, cells)]
    scratch += [
        pltpu.SemaphoreType.DMA((32,)), pltpu.SemaphoreType.DMA((160,)), pltpu.SemaphoreType.DMA((160,)),
    ]
    results = ((weights.shape, BF16), (small, F32), (small, F32), (small, F32))
    held = pl.pallas_call(
        kernel,
        out_shape=tuple(vmem(*r) for r in results),
        in_specs=[pl.BlockSpec(memory_space=pltpu.HBM)] * 6,
        out_specs=(pl.BlockSpec(memory_space=vmem),) * 4,
        scratch_shapes=scratch,
        compiler_params=pltpu.CompilerParams(
            collective_id=0, has_side_effects=True, vmem_limit_bytes=60 << 20
        ),
        name="lowrank_adam",
    )(activations, signals, projectors, weights, first_moment, second_moment)
    held = [pltpu.with_memory_space_constraint(h, vmem) for h in held]
    return pl.pallas_call(
        write_out,
        out_shape=tuple(jax.ShapeDtypeStruct(*r) for r in results),
        in_specs=[pl.BlockSpec(memory_space=vmem)] * 4,
        out_specs=(pl.BlockSpec(memory_space=pltpu.HBM),) * 4,
        scratch_shapes=[pltpu.SemaphoreType.DMA((4,))],
        name="write_out",
    )(*held)


def solution(mesh):
    split = P(None, "dp", "tensor")
    return jax.shard_map(
        on_device,
        mesh=mesh,
        in_specs=(split, split, P(), split, split, split),
        out_specs=(split, split, split, split),
        check_vma=False,
    )
```

```python
import functools

import jax
import jax.numpy as jnp
from jax import lax
from jax.experimental import pallas as pl
from jax.experimental.pallas import tpu as pltpu
from jax.sharding import PartitionSpec as P

MESH = pl.DeviceIdType.MESH
F32, BF16 = jnp.float32, jnp.bfloat16

beta_one = 0.9
beta_two = 0.999
adam_step = 1000
adam_eps = 1e-08
learning_rate = 0.05
first_fix = 1.0 - beta_one**adam_step
second_fix = 1.0 - beta_two**adam_step

NZ, NX, NY = 8, 2, 4
SIZES = {"z": NZ, "y": NY, "x": NX, "xy": NX * NY}
AROUND, ACROSS, ALONG = ("z", "xy"), ("y", "x", "z"), ("x", "y", "z")
PARTS = (
    (0, 0, 1280, ALONG),
    (0, 1280, 1472, ACROSS),
    (1, 0, 1024, ALONG),
    (1, 1024, 1728, AROUND),
    (2, 0, 1024, ALONG),
    (2, 1024, 1728, ACROSS),
)
BLOCK = 512


def blocks(width):
    return [(at, min(BLOCK, width - at)) for at in range(0, width, BLOCK)]


def route_rows(route):
    return tuple(SIZES[g] for g in route[:-1])


def permutation(route, count):
    p = lax.broadcasted_iota(jnp.int32, (count, count), 0)
    r = lax.broadcasted_iota(jnp.int32, (count, count), 1)
    parts, rest = {}, p // 2
    for g in reversed(route):
        parts[g] = rest % SIZES[g]
        rest = rest // SIZES[g]
    if "xy" in parts:
        parts["x"], parts["y"] = parts["xy"] // NY, parts["xy"] % NY
    natural = ((parts["z"] * NX + parts["x"]) * NY + parts["y"]) * 2 + p % 2
    return (natural == r).astype(F32).astype(BF16)


def kernel(
    act, sig, proj, weights, first, second,
    new_weights, new_first, new_second, new_dir,
    act_v, sig_v, p_v, ploc_v, w_v, m1_v, m2_v, qp, rc, sx, rx, q_v, *rest,
):
    n = len(PARTS)
    grads, firsts, seconds, second_recv, sl, rl, gl, dirs = (rest[i * n : (i + 1) * n] for i in range(8))
    lsem, ssem, rsem = rest[8 * n :]
    dp, tp = lax.axis_index("dp"), lax.axis_index("tensor")
    z, xl, y = dp // (NX * NY), (dp // NY) % NX, dp % NY
    xh, core = tp // 2, tp % 2
    tokens, depth = act_v.shape[1], act_v.shape[2]
    width = sig_v.shape[1]
    half = tokens // 2
    rows = w_v.shape[1]

    def device(zz, xx, yy, hh=None, cc=None):
        hh = xh if hh is None else hh
        cc = core if cc is None else cc
        return ((zz * NX + xx) * NY + yy, hh * 2 + cc)

    index = {"z": z, "y": y, "x": xl, "xy": xl * NY + y}

    def peer(group, d):
        if group == "z":
            to, frm = (z + d) % NZ, (z + NZ - d) % NZ
            return device(to, xl, y), to, frm
        if group == "y":
            to, frm = (y + d) % NY, (y + NY - d) % NY
            return device(z, xl, to), to, frm
        if group == "x":
            return device(z, 1 - xl, y), 1 - xl, 1 - xl
        dx, dy = d // NY, d % NY
        xx = 1 - xl if dx else xl
        to, frm = (y + dy) % NY, (y + NY - dy) % NY
        return device(z, xx, to), xx * NY + to, xx * NY + frm

    core_peer = device(z, xl, y, xh, 1 - core)
    high_peer = device(z, xl, y, 1 - xh, core)

    loads = {}

    def load(name, src, dst):
        c = pltpu.make_async_copy(src, dst, lsem.at[len(loads)])
        c.start()
        loads[name] = c

    part = pl.ds(pl.multiple_of(tp * depth, depth), depth)
    load("a0", act.at[0], act_v.at[0])
    load("p0", proj.at[0, part], p_v.at[0])
    load("p1", proj.at[1, part], p_v.at[1])

    def load_rest():
        load("a1", act.at[1], act_v.at[1])
        load("p2", proj.at[2, part], p_v.at[2])
        for k in range(3):
            load(f"s{k}", sig.at[k], sig_v.at[k])
        own = pl.ds(pl.multiple_of(dp * rows, rows), rows)
        load("pl", proj.at[:, own], ploc_v)
        load("m1", first, m1_v)
        load("m2", second, m2_v)
        load("w", weights, w_v)


    barrier = pltpu.get_barrier_semaphore()
    partners = [core_peer, high_peer]
    partners += [peer("z", d)[0] for d in range(1, NZ)]
    partners += [peer("xy", d)[0] for d in range(1, NX * NY)]
    for p in partners:
        pl.semaphore_signal(barrier, inc=1, device_id=p, device_id_type=MESH)

    sends = []

    def remote(src, dst, sem, to):
        return pltpu.make_async_remote_copy(
            src_ref=src, dst_ref=dst, send_sem=ssem.at[sem], recv_sem=rsem.at[sem],
            device_id=to, device_id_type=MESH,
        )

    def send(src, dst, sem, to):
        c = remote(src, dst, sem, to)
        c.start()
        sends.append(c)

    def send_all(copies, whole, sem):
        for src, dst, to in copies:
            remote(src, dst, sem, to).start()
        sends.append(remote(whole, whole, sem, copies[0][2]))

    counter = [0]

    def sems(n):
        counter[0] += n
        return counter[0] - n

    core_one, high_one, core_two = sems(3), sems(3), sems(3)

    def project(k):
        source = (0, 0, 1)[k]
        value = jnp.dot(act_v[source], p_v[k], preferred_element_type=F32)
        qp[k] = value.reshape(2, half, value.shape[1])

    perms = {route: permutation(route, 128) for route in {p[3]: 0 for p in PARTS}}
    base = [[sems(1) for g in p[3]] for p in PARTS]
    base_back = [[sems(1) for g in p[3]] for p in PARTS]

    def core_send(k):
        if k != 1:
            loads[("a0", "", "a1")[k]].wait()
        loads[f"p{k}"].wait()
        if k == 0:
            load_rest()
        project(k)
        if k == 0:
            pl.semaphore_wait(barrier, len(partners))
        send(qp.at[k, 1 - core], rc.at[k], core_one + k, core_peer)

    def high_send(k):
        remote(qp.at[k, 0], rc.at[k], core_one + k, core_peer).wait_recv()
        total = qp[k, core] + rc[k]
        rc[k] = total
        sx[k] = total.astype(BF16)
        send(sx.at[k], rx.at[k], high_one + k, high_peer)

    def core_back(k):
        remote(sx.at[k], rx.at[k], high_one + k, high_peer).wait_recv()
        q_v[k, core] = (rc[k] + rx[k].astype(F32)).astype(BF16)
        send(q_v.at[k, core], q_v.at[k, core], core_two + k, core_peer)

    def partners_of(p, stage):
        group = PARTS[p][3][stage]
        return [peer(group, d) for d in range(1, SIZES[group])]

    def scatter(p, stage, src, recv):
        copies = [(src.at[idx], recv.at[i], to) for i, (to, idx, _) in enumerate(partners_of(p, stage))]
        send_all(copies, src.at[pl.ds(0, len(copies))], base[p][stage])

    def arrived(p, stage, src, recv):
        to = partners_of(p, stage)[0][0]
        remote(recv, recv, base[p][stage], to).wait_recv()

    def gradient_of(k):
        remote(q_v.at[k, 1 - core], q_v.at[k, 1 - core], core_two + k, core_peer).wait_recv()
        q = q_v[k].reshape(tokens, 128)
        loads[f"s{k}"].wait()
        for p, part in enumerate(PARTS):
            if part[0] != k:
                continue
            turned = lax.dot_general(
                perms[part[3]], q, (((1,), (1,)), ((), ())), preferred_element_type=F32
            ).astype(BF16)
            start, size = part[1:3]
            lead = grads[p].shape[:-1]
            for at, w in blocks(size):
                value = lax.dot_general(
                    turned, sig_v[k, start + at : start + at + w, :], (((1,), (1,)), ((), ())),
                    preferred_element_type=F32,
                )
                grads[p][..., at : at + w] = value.astype(BF16).reshape(lead + (w,))
            scatter(p, 0, grads[p], firsts[p])

    def summed(src, recv, idx, at, w):
        total = src[idx, ..., at : at + w].astype(F32)
        for i in range(recv.shape[0]):
            total = total + recv[i, ..., at : at + w].astype(F32)
        return total

    def to_pieces(p, total, at, w):
        for i in range(8):
            sl[p][i, :, at : at + w] = total[2 * i : 2 * i + 2].astype(BF16)

    def first_sum(p):
        route = PARTS[p][3]
        arrived(p, 0, grads[p], firsts[p])
        for at, w in blocks(PARTS[p][2]):
            total = summed(grads[p], firsts[p], index[route[0]], at, w)
            if len(route) == 2:
                to_pieces(p, total, at, w)
            else:
                seconds[p][:, :, at : at + w] = total.astype(BF16)
        if len(route) == 2:
            scatter(p, 1, sl[p], rl[p])
        else:
            scatter(p, 1, seconds[p], second_recv[p])

    def second_sum(p):
        route = PARTS[p][3]
        if len(route) == 2:
            return
        arrived(p, 1, seconds[p], second_recv[p])
        for at, w in blocks(PARTS[p][2]):
            to_pieces(p, summed(seconds[p], second_recv[p], index[route[1]], at, w), at, w)
        scatter(p, 2, sl[p], rl[p])

    count = float(tokens * NZ * NX * NY)

    def update(p):
        k, _, _, route = PARTS[p]
        last = len(route) - 1
        arrived(p, last, sl[p], rl[p])
        idx = index[route[last]]
        start, size = PARTS[p][1:3]
        for at, w in blocks(size):
            cols = slice(start + at, start + at + w)
            gradient = summed(sl[p], rl[p], idx, at, w) / count
            one = beta_one * m1_v[k, :, cols] + (1.0 - beta_one) * gradient
            two = beta_two * m2_v[k, :, cols] + (1.0 - beta_two) * gradient * gradient
            heading = one / first_fix / (jnp.sqrt(two / second_fix) + adam_eps)
            new_first[k, :, cols] = one
            new_second[k, :, cols] = two
            new_dir[k, :, cols] = heading
            gl[p][idx, :, at : at + w] = heading.astype(BF16)
        copies = [(gl[p].at[idx], gl[p].at[idx], to) for to, _, _ in partners_of(p, last)]
        send_all(copies, gl[p].at[pl.ds(0, 7)], base_back[p][last])

    def place(p, stage):
        return tuple(index[g] for g in PARTS[p][3][: stage + 1])

    def others(p, stage):
        lead = place(p, stage)[:-1]
        return dirs[p].at[lead + (pl.ds(0, SIZES[PARTS[p][3][stage]] - 1),)]

    def spread(p, stage):
        slot = dirs[p].at[place(p, stage)]
        copies = [(slot, slot, to) for to, _, _ in partners_of(p, stage)]
        send_all(copies, others(p, stage), base_back[p][stage])

    def gathered(p, stage):
        to = partners_of(p, stage)[0][0]
        remote(others(p, stage), others(p, stage), base_back[p][stage], to).wait_recv()

    def joined(p):
        route = PARTS[p][3]
        last = len(route) - 1
        seven = gl[p].at[pl.ds(0, 7)]
        remote(seven, seven, base_back[p][last], partners_of(p, last)[0][0]).wait_recv()
        at16 = place(p, last - 1)
        for at, w in blocks(PARTS[p][2]):
            pieces = [gl[p][i, :, at : at + w].astype(F32) for i in range(8)]
            dirs[p][at16 + (slice(None), slice(at, at + w))] = jnp.concatenate(pieces, axis=0).astype(BF16)
        spread(p, last - 1)

    def middle(p):
        if len(PARTS[p][3]) == 3:
            gathered(p, 1)
            spread(p, 0)

    def finish(p):
        k, _, _, route = PARTS[p]
        gathered(p, 0)
        basis = lax.dot_general(
            ploc_v[k], perms[route], (((1,), (1,)), ((), ())), preferred_element_type=F32
        ).astype(BF16)
        start, size = PARTS[p][1:3]
        for at, w in blocks(size):
            cols = slice(start + at, start + at + w)
            heading = dirs[p][..., at : at + w].reshape(128, w)
            change = jnp.dot(basis, heading, preferred_element_type=F32)
            new_weights[k, :, cols] = (w_v[k, :, cols].astype(F32) - learning_rate * change).astype(BF16)

    core_send(0)
    core_send(1)
    high_send(0)
    core_send(2)
    high_send(1)
    high_send(2)
    core_back(0)
    core_back(1)
    gradient_of(0)
    core_back(2)
    gradient_of(1)
    gradient_of(2)

    for name in ("m1", "m2", "pl", "w"):
        loads[name].wait()
    for op, p in (
        (first_sum, 1), (first_sum, 0), (first_sum, 2), (first_sum, 4), (first_sum, 5), (second_sum, 1),
        (second_sum, 0), (second_sum, 2), (second_sum, 5), (first_sum, 3), (second_sum, 4), (update, 1),
        (update, 0), (update, 2), (update, 3), (update, 5), (update, 4), (joined, 0),
        (joined, 3), (joined, 1), (joined, 2), (joined, 5), (joined, 4), (middle, 1),
        (middle, 0), (middle, 2), (middle, 5), (middle, 4), (finish, 0), (finish, 2),
        (finish, 1), (finish, 3), (finish, 4), (finish, 5),
    ):
        op(p)
    for c in sends:
        c.wait_send()


def write_out(*refs):
    sem = refs[8]
    copies = [pltpu.make_async_copy(refs[i], refs[4 + i], sem.at[i]) for i in range(4)]
    for c in copies:
        c.start()
    for c in copies:
        c.wait()


def on_device(activations, signals, projectors, weights, first_moment, second_moment):
    signals = jnp.transpose(signals, (0, 2, 1))
    _, tokens, depth = activations.shape
    _, width, _ = signals.shape
    rank = projectors.shape[2]
    rows = weights.shape[1]
    half = tokens // 2
    small = first_moment.shape
    vmem = pltpu.VMEM
    lead = [route_rows(p[3]) for p in PARTS]
    cells = [(16, p[2]) for p in PARTS]

    def small_like(n):
        return [vmem((n, 2, c[1]), BF16) for c in cells]

    scratch = [
        vmem(activations.shape, BF16), vmem(signals.shape, BF16), vmem((3, depth, rank), BF16),
        vmem((3, rows, rank), BF16), vmem(weights.shape, BF16), vmem(small, F32), vmem(small, F32),
        vmem((3, 2, half, rank), F32), vmem((3, half, rank), F32), vmem((3, half, rank), BF16),
        vmem((3, half, rank), BF16), vmem((3, 2, half, rank), BF16),
    ]
    scratch += [vmem(l + c, BF16) for l, c in zip(lead, cells)]
    scratch += [vmem((l[0] - 1,) + l[1:] + c, BF16) for l, c in zip(lead, cells)]
    scratch += [vmem((l + (1,))[1:2] + c, BF16) for l, c in zip(lead, cells)]
    scratch += [vmem((max((l + (1,))[1] - 1, 1),) + c, BF16) for l, c in zip(lead, cells)]
    scratch += small_like(8) + small_like(7) + small_like(8)
    scratch += [vmem(l + c, BF16) for l, c in zip(lead, cells)]
    n_sem = 9 + 2 * sum(len(p[3]) for p in PARTS)
    scratch += [
        pltpu.SemaphoreType.DMA((12,)), pltpu.SemaphoreType.DMA((n_sem,)), pltpu.SemaphoreType.DMA((n_sem,)),
    ]
    results = ((weights.shape, BF16), (small, F32), (small, F32), (small, F32))
    held = pl.pallas_call(
        kernel,
        out_shape=tuple(vmem(*r) for r in results),
        in_specs=[pl.BlockSpec(memory_space=pltpu.HBM)] * 6,
        out_specs=(pl.BlockSpec(memory_space=vmem),) * 4,
        scratch_shapes=scratch,
        compiler_params=pltpu.CompilerParams(
            collective_id=0, has_side_effects=True, vmem_limit_bytes=60 << 20
        ),
        name="lowrank_adam",
    )(activations, signals, projectors, weights, first_moment, second_moment)
    held = [pltpu.with_memory_space_constraint(h, vmem) for h in held]
    return pl.pallas_call(
        write_out,
        out_shape=tuple(jax.ShapeDtypeStruct(*r) for r in results),
        in_specs=[pl.BlockSpec(memory_space=vmem)] * 4,
        out_specs=(pl.BlockSpec(memory_space=pltpu.HBM),) * 4,
        scratch_shapes=[pltpu.SemaphoreType.DMA((4,))],
        name="write_out",
    )(*held)


def solution(mesh):
    split = P(None, "dp", "tensor")
    return jax.shard_map(
        on_device,
        mesh=mesh,
        in_specs=(split, split, P(), split, split, split),
        out_specs=(split, split, split, split),
        check_vma=False,
    )
```

```python
import functools

import jax
import jax.numpy as jnp
from jax import lax
from jax.experimental import pallas as pl
from jax.experimental.pallas import tpu as pltpu
from jax.sharding import PartitionSpec as P

MESH = pl.DeviceIdType.MESH
F32, BF16 = jnp.float32, jnp.bfloat16

beta_one = 0.9
beta_two = 0.999
adam_step = 1000
adam_eps = 1e-08
learning_rate = 0.05
first_fix = 1.0 - beta_one**adam_step
second_fix = 1.0 - beta_two**adam_step

NZ, NX, NY = 8, 2, 4
SIZES = {"z": NZ, "y": NY, "x": NX, "xy": NX * NY}
AROUND, ACROSS, ALONG = ("z", "xy"), ("y", "x", "z"), ("x", "y", "z")
PARTS = (
    (0, 0, 1280, ALONG),
    (0, 1280, 1472, ACROSS),
    (1, 0, 1024, ALONG),
    (1, 1024, 1728, AROUND),
    (2, 0, 1024, ALONG),
    (2, 1024, 1728, ACROSS),
)
BLOCK = 512


def blocks(width):
    return [(at, min(BLOCK, width - at)) for at in range(0, width, BLOCK)]


def route_rows(route):
    return tuple(SIZES[g] for g in route[:-1])


def permutation(route, count):
    p = lax.broadcasted_iota(jnp.int32, (count, count), 0)
    r = lax.broadcasted_iota(jnp.int32, (count, count), 1)
    parts, rest = {}, p // 2
    for g in reversed(route):
        parts[g] = rest % SIZES[g]
        rest = rest // SIZES[g]
    if "xy" in parts:
        parts["x"], parts["y"] = parts["xy"] // NY, parts["xy"] % NY
    natural = ((parts["z"] * NX + parts["x"]) * NY + parts["y"]) * 2 + p % 2
    return (natural == r).astype(F32).astype(BF16)


def kernel(
    act, sig, proj, weights, first, second,
    new_weights, new_first, new_second, new_dir,
    act_v, sig_v, p_v, ploc_v, w_v, m1_v, m2_v, qp, rc, sx, rx, q_v, *rest,
):
    n = len(PARTS)
    grads, firsts, seconds, second_recv, sl, rl, gl, dirs = (rest[i * n : (i + 1) * n] for i in range(8))
    lsem, ssem, rsem, ready = rest[8 * n :]
    dp, tp = lax.axis_index("dp"), lax.axis_index("tensor")
    z, xl, y = dp // (NX * NY), (dp // NY) % NX, dp % NY
    xh, core = tp // 2, tp % 2
    tokens, depth = act_v.shape[1], act_v.shape[2]
    width = sig_v.shape[1]
    half = tokens // 2
    rows = w_v.shape[1]

    def device(zz, xx, yy, hh=None, cc=None):
        hh = xh if hh is None else hh
        cc = core if cc is None else cc
        return ((zz * NX + xx) * NY + yy, hh * 2 + cc)

    index = {"z": z, "y": y, "x": xl, "xy": xl * NY + y}

    def peer(group, d):
        if group == "z":
            to, frm = (z + d) % NZ, (z + NZ - d) % NZ
            return device(to, xl, y), to, frm
        if group == "y":
            to, frm = (y + d) % NY, (y + NY - d) % NY
            return device(z, xl, to), to, frm
        if group == "x":
            return device(z, 1 - xl, y), 1 - xl, 1 - xl
        dx, dy = d // NY, d % NY
        xx = 1 - xl if dx else xl
        to, frm = (y + dy) % NY, (y + NY - dy) % NY
        return device(z, xx, to), xx * NY + to, xx * NY + frm

    core_peer = device(z, xl, y, xh, 1 - core)
    high_peer = device(z, xl, y, 1 - xh, core)

    barrier = pltpu.get_barrier_semaphore()
    along_z = [peer("z", d)[0] for d in (1, NZ - 1)]
    along_y = [peer("y", d)[0] for d in (1, NY - 1)]
    partners = [core_peer, high_peer, peer("x", 1)[0]] + along_z + along_y
    for p in partners:
        pl.semaphore_signal(barrier, inc=1, device_id=p, device_id_type=MESH)
    rounds = (along_z + along_y, along_z + along_y, along_z)

    def tell(i):
        for p in rounds[i]:
            pl.semaphore_signal(ready.at[i], inc=1, device_id=p, device_id_type=MESH)

    def told(i):
        pl.semaphore_wait(ready.at[i], len(rounds[i]))

    loads = {}

    def load(name, src, dst):
        c = pltpu.make_async_copy(src, dst, lsem.at[len(loads)])
        c.start()
        loads[name] = c

    part = pl.ds(pl.multiple_of(tp * depth, depth), depth)
    load("a0", act.at[0], act_v.at[0])
    load("p0", proj.at[0, part], p_v.at[0])
    load("p1", proj.at[1, part], p_v.at[1])

    def load_rest():
        load("a1", act.at[1], act_v.at[1])
        load("p2", proj.at[2, part], p_v.at[2])
        for k in range(3):
            load(f"s{k}", sig.at[k], sig_v.at[k])
        own = pl.ds(pl.multiple_of(dp * rows, rows), rows)
        load("pl", proj.at[:, own], ploc_v)
        load("m1", first, m1_v)
        load("m2", second, m2_v)
        load("w", weights, w_v)


    sends = []

    def remote(src, dst, sem, to):
        return pltpu.make_async_remote_copy(
            src_ref=src, dst_ref=dst, send_sem=ssem.at[sem], recv_sem=rsem.at[sem],
            device_id=to, device_id_type=MESH,
        )

    def send(src, dst, sem, to):
        c = remote(src, dst, sem, to)
        c.start()
        sends.append(c)

    def send_all(copies, whole, sem):
        for src, dst, to in copies:
            remote(src, dst, sem, to).start()
        sends.append(remote(whole, whole, sem, copies[0][2]))

    counter = [0]

    def sems(n):
        counter[0] += n
        return counter[0] - n

    core_one, high_one, core_two = sems(3), sems(3), sems(3)

    def project(k):
        source = (0, 0, 1)[k]
        value = jnp.dot(act_v[source], p_v[k], preferred_element_type=F32)
        qp[k] = value.reshape(2, half, value.shape[1])

    perms = {route: permutation(route, 128) for route in {p[3]: 0 for p in PARTS}}
    base = [[sems(1) for g in p[3]] for p in PARTS]
    base_back = [[sems(1) for g in p[3]] for p in PARTS]

    def core_send(k):
        if k != 1:
            loads[("a0", "", "a1")[k]].wait()
        loads[f"p{k}"].wait()
        if k == 0:
            load_rest()
        project(k)
        if k == 0:
            pl.semaphore_wait(barrier, len(partners))
        send(qp.at[k, 1 - core], rc.at[k], core_one + k, core_peer)

    def high_send(k):
        remote(qp.at[k, 0], rc.at[k], core_one + k, core_peer).wait_recv()
        total = qp[k, core] + rc[k]
        rc[k] = total
        sx[k] = total.astype(BF16)
        send(sx.at[k], rx.at[k], high_one + k, high_peer)

    def core_back(k):
        remote(sx.at[k], rx.at[k], high_one + k, high_peer).wait_recv()
        q_v[k, core] = (rc[k] + rx[k].astype(F32)).astype(BF16)
        send(q_v.at[k, core], q_v.at[k, core], core_two + k, core_peer)

    def partners_of(p, stage):
        group = PARTS[p][3][stage]
        return [peer(group, d) for d in range(1, SIZES[group])]

    def scatter(p, stage, src, recv):
        copies = [(src.at[idx], recv.at[i], to) for i, (to, idx, _) in enumerate(partners_of(p, stage))]
        send_all(copies, src.at[pl.ds(0, len(copies))], base[p][stage])

    def arrived(p, stage, src, recv):
        to = partners_of(p, stage)[0][0]
        remote(recv, recv, base[p][stage], to).wait_recv()

    def gradient_of(k):
        remote(q_v.at[k, 1 - core], q_v.at[k, 1 - core], core_two + k, core_peer).wait_recv()
        q = q_v[k].reshape(tokens, 128)
        loads[f"s{k}"].wait()
        for p, part in enumerate(PARTS):
            if part[0] != k:
                continue
            turned = lax.dot_general(
                perms[part[3]], q, (((1,), (1,)), ((), ())), preferred_element_type=F32
            ).astype(BF16)
            start, size = part[1:3]
            lead = grads[p].shape[:-1]
            for at, w in blocks(size):
                value = lax.dot_general(
                    turned, sig_v[k, start + at : start + at + w, :], (((1,), (1,)), ((), ())),
                    preferred_element_type=F32,
                )
                grads[p][..., at : at + w] = value.astype(BF16).reshape(lead + (w,))
            scatter(p, 0, grads[p], firsts[p])

    def summed(src, recv, idx, at, w):
        total = src[idx, ..., at : at + w].astype(F32)
        for i in range(recv.shape[0]):
            total = total + recv[i, ..., at : at + w].astype(F32)
        return total

    def to_pieces(p, total, at, w):
        for i in range(8):
            sl[p][i, :, at : at + w] = total[2 * i : 2 * i + 2].astype(BF16)

    def first_sum(p):
        route = PARTS[p][3]
        arrived(p, 0, grads[p], firsts[p])
        for at, w in blocks(PARTS[p][2]):
            total = summed(grads[p], firsts[p], index[route[0]], at, w)
            if len(route) == 2:
                to_pieces(p, total, at, w)
            else:
                seconds[p][:, :, at : at + w] = total.astype(BF16)
        if len(route) == 2:
            scatter(p, 1, sl[p], rl[p])
        else:
            scatter(p, 1, seconds[p], second_recv[p])

    def second_sum(p):
        route = PARTS[p][3]
        if len(route) == 2:
            return
        arrived(p, 1, seconds[p], second_recv[p])
        for at, w in blocks(PARTS[p][2]):
            to_pieces(p, summed(seconds[p], second_recv[p], index[route[1]], at, w), at, w)
        scatter(p, 2, sl[p], rl[p])

    count = float(tokens * NZ * NX * NY)

    def update(p):
        k, _, _, route = PARTS[p]
        last = len(route) - 1
        arrived(p, last, sl[p], rl[p])
        idx = index[route[last]]
        start, size = PARTS[p][1:3]
        for at, w in blocks(size):
            cols = slice(start + at, start + at + w)
            gradient = summed(sl[p], rl[p], idx, at, w) / count
            one = beta_one * m1_v[k, :, cols] + (1.0 - beta_one) * gradient
            two = beta_two * m2_v[k, :, cols] + (1.0 - beta_two) * gradient * gradient
            heading = one / first_fix / (jnp.sqrt(two / second_fix) + adam_eps)
            new_first[k, :, cols] = one
            new_second[k, :, cols] = two
            new_dir[k, :, cols] = heading
            gl[p][idx, :, at : at + w] = heading.astype(BF16)
        copies = [(gl[p].at[idx], gl[p].at[idx], to) for to, _, _ in partners_of(p, last)]
        send_all(copies, gl[p].at[pl.ds(0, 7)], base_back[p][last])

    def place(p, stage):
        return tuple(index[g] for g in PARTS[p][3][: stage + 1])

    def others(p, stage):
        lead = place(p, stage)[:-1]
        return dirs[p].at[lead + (pl.ds(0, SIZES[PARTS[p][3][stage]] - 1),)]

    def spread(p, stage):
        slot = dirs[p].at[place(p, stage)]
        copies = [(slot, slot, to) for to, _, _ in partners_of(p, stage)]
        send_all(copies, others(p, stage), base_back[p][stage])

    def gathered(p, stage):
        to = partners_of(p, stage)[0][0]
        remote(others(p, stage), others(p, stage), base_back[p][stage], to).wait_recv()

    def joined(p):
        route = PARTS[p][3]
        last = len(route) - 1
        seven = gl[p].at[pl.ds(0, 7)]
        remote(seven, seven, base_back[p][last], partners_of(p, last)[0][0]).wait_recv()
        at16 = place(p, last - 1)
        for at, w in blocks(PARTS[p][2]):
            pieces = [gl[p][i, :, at : at + w].astype(F32) for i in range(8)]
            dirs[p][at16 + (slice(None), slice(at, at + w))] = jnp.concatenate(pieces, axis=0).astype(BF16)
        spread(p, last - 1)

    def middle(p):
        if len(PARTS[p][3]) == 3:
            gathered(p, 1)
            spread(p, 0)

    def finish(p):
        k, _, _, route = PARTS[p]
        gathered(p, 0)
        basis = lax.dot_general(
            ploc_v[k], perms[route], (((1,), (1,)), ((), ())), preferred_element_type=F32
        ).astype(BF16)
        start, size = PARTS[p][1:3]
        for at, w in blocks(size):
            cols = slice(start + at, start + at + w)
            heading = dirs[p][..., at : at + w].reshape(128, w)
            change = jnp.dot(basis, heading, preferred_element_type=F32)
            new_weights[k, :, cols] = (w_v[k, :, cols].astype(F32) - learning_rate * change).astype(BF16)

    core_send(0)
    tell(0)
    core_send(1)
    high_send(0)
    told(0)
    tell(1)
    core_send(2)
    high_send(1)
    high_send(2)
    told(1)
    tell(2)
    core_back(0)
    core_back(1)
    told(2)
    gradient_of(0)
    core_back(2)
    gradient_of(1)
    gradient_of(2)

    for name in ("m1", "m2", "pl", "w"):
        loads[name].wait()
    for op, p in (
        (first_sum, 1), (first_sum, 0), (first_sum, 2), (first_sum, 4), (first_sum, 5), (second_sum, 1),
        (second_sum, 0), (second_sum, 2), (second_sum, 5), (first_sum, 3), (second_sum, 4), (update, 1),
        (update, 0), (update, 2), (update, 3), (update, 5), (update, 4), (joined, 0),
        (joined, 3), (joined, 1), (joined, 2), (joined, 5), (joined, 4), (middle, 1),
        (middle, 0), (middle, 2), (middle, 5), (middle, 4), (finish, 0), (finish, 2),
        (finish, 1), (finish, 3), (finish, 4), (finish, 5),
    ):
        op(p)
    for c in sends:
        c.wait_send()


def write_out(*refs):
    sem = refs[8]
    copies = [pltpu.make_async_copy(refs[i], refs[4 + i], sem.at[i]) for i in range(4)]
    for c in copies:
        c.start()
    for c in copies:
        c.wait()


def on_device(activations, signals, projectors, weights, first_moment, second_moment):
    signals = jnp.transpose(signals, (0, 2, 1))
    _, tokens, depth = activations.shape
    _, width, _ = signals.shape
    rank = projectors.shape[2]
    rows = weights.shape[1]
    half = tokens // 2
    small = first_moment.shape
    vmem = pltpu.VMEM
    lead = [route_rows(p[3]) for p in PARTS]
    cells = [(16, p[2]) for p in PARTS]

    def small_like(n):
        return [vmem((n, 2, c[1]), BF16) for c in cells]

    scratch = [
        vmem(activations.shape, BF16), vmem(signals.shape, BF16), vmem((3, depth, rank), BF16),
        vmem((3, rows, rank), BF16), vmem(weights.shape, BF16), vmem(small, F32), vmem(small, F32),
        vmem((3, 2, half, rank), F32), vmem((3, half, rank), F32), vmem((3, half, rank), BF16),
        vmem((3, half, rank), BF16), vmem((3, 2, half, rank), BF16),
    ]
    scratch += [vmem(l + c, BF16) for l, c in zip(lead, cells)]
    scratch += [vmem((l[0] - 1,) + l[1:] + c, BF16) for l, c in zip(lead, cells)]
    scratch += [vmem((l + (1,))[1:2] + c, BF16) for l, c in zip(lead, cells)]
    scratch += [vmem((max((l + (1,))[1] - 1, 1),) + c, BF16) for l, c in zip(lead, cells)]
    scratch += small_like(8) + small_like(7) + small_like(8)
    scratch += [vmem(l + c, BF16) for l, c in zip(lead, cells)]
    n_sem = 9 + 2 * sum(len(p[3]) for p in PARTS)
    scratch += [
        pltpu.SemaphoreType.DMA((12,)), pltpu.SemaphoreType.DMA((n_sem,)), pltpu.SemaphoreType.DMA((n_sem,)),
        pltpu.SemaphoreType.REGULAR((3,)),
    ]
    results = ((weights.shape, BF16), (small, F32), (small, F32), (small, F32))
    held = pl.pallas_call(
        kernel,
        out_shape=tuple(vmem(*r) for r in results),
        in_specs=[pl.BlockSpec(memory_space=pltpu.HBM)] * 6,
        out_specs=(pl.BlockSpec(memory_space=vmem),) * 4,
        scratch_shapes=scratch,
        compiler_params=pltpu.CompilerParams(
            collective_id=0, has_side_effects=True, vmem_limit_bytes=60 << 20
        ),
        name="lowrank_adam",
    )(activations, signals, projectors, weights, first_moment, second_moment)
    held = [pltpu.with_memory_space_constraint(h, vmem) for h in held]
    return pl.pallas_call(
        write_out,
        out_shape=tuple(jax.ShapeDtypeStruct(*r) for r in results),
        in_specs=[pl.BlockSpec(memory_space=vmem)] * 4,
        out_specs=(pl.BlockSpec(memory_space=pltpu.HBM),) * 4,
        scratch_shapes=[pltpu.SemaphoreType.DMA((4,))],
        name="write_out",
    )(*held)


def solution(mesh):
    split = P(None, "dp", "tensor")
    return jax.shard_map(
        on_device,
        mesh=mesh,
        in_specs=(split, split, P(), split, split, split),
        out_specs=(split, split, split, split),
        check_vma=False,
    )
```

```python
import functools

import jax
import jax.numpy as jnp
from jax import lax
from jax.experimental import pallas as pl
from jax.experimental.pallas import tpu as pltpu
from jax.sharding import PartitionSpec as P

MESH = pl.DeviceIdType.MESH
F32, BF16 = jnp.float32, jnp.bfloat16

beta_one = 0.9
beta_two = 0.999
adam_step = 1000
adam_eps = 1e-08
learning_rate = 0.05
first_fix = 1.0 - beta_one**adam_step
second_fix = 1.0 - beta_two**adam_step

NZ, NX, NY = 8, 2, 4
SIZES = {"z": NZ, "y": NY, "x": NX, "xy": NX * NY}
AROUND, ACROSS, ALONG = ("z", "xy"), ("y", "x", "z"), ("x", "y", "z")
PARTS = (
    (0, 0, 1280, ALONG),
    (0, 1280, 1472, ACROSS),
    (1, 0, 1024, ALONG),
    (1, 1024, 1728, AROUND),
    (2, 0, 1024, ALONG),
    (2, 1024, 1728, ACROSS),
)
BLOCK = 512


def blocks(width):
    return [(at, min(BLOCK, width - at)) for at in range(0, width, BLOCK)]


def route_rows(route):
    return tuple(SIZES[g] for g in route[:-1])


def permutation(route, count):
    p = lax.broadcasted_iota(jnp.int32, (count, count), 0)
    r = lax.broadcasted_iota(jnp.int32, (count, count), 1)
    parts, rest = {}, p // 2
    for g in reversed(route):
        parts[g] = rest % SIZES[g]
        rest = rest // SIZES[g]
    if "xy" in parts:
        parts["x"], parts["y"] = parts["xy"] // NY, parts["xy"] % NY
    natural = ((parts["z"] * NX + parts["x"]) * NY + parts["y"]) * 2 + p % 2
    return (natural == r).astype(F32).astype(BF16)


def kernel(
    act, sig, proj, weights, first, second,
    new_weights, new_first, new_second, new_dir,
    act_v, sig_v, p_v, ploc_v, w_v, m1_v, m2_v, qp, rc, sx, rx, q_v, *rest,
):
    n = len(PARTS)
    grads, firsts, seconds, second_recv, sl, rl, gl, dirs = (rest[i * n : (i + 1) * n] for i in range(8))
    lsem, ssem, rsem, ready = rest[8 * n :]
    dp, tp = lax.axis_index("dp"), lax.axis_index("tensor")
    z, xl, y = dp // (NX * NY), (dp // NY) % NX, dp % NY
    xh, core = tp // 2, tp % 2
    tokens, depth = act_v.shape[1], act_v.shape[2]
    width = sig_v.shape[1]
    half = tokens // 2
    rows = w_v.shape[1]

    def device(zz, xx, yy, hh=None, cc=None):
        hh = xh if hh is None else hh
        cc = core if cc is None else cc
        return ((zz * NX + xx) * NY + yy, hh * 2 + cc)

    index = {"z": z, "y": y, "x": xl, "xy": xl * NY + y}

    def peer(group, d):
        if group == "z":
            to, frm = (z + d) % NZ, (z + NZ - d) % NZ
            return device(to, xl, y), to, frm
        if group == "y":
            to, frm = (y + d) % NY, (y + NY - d) % NY
            return device(z, xl, to), to, frm
        if group == "x":
            return device(z, 1 - xl, y), 1 - xl, 1 - xl
        dx, dy = d // NY, d % NY
        xx = 1 - xl if dx else xl
        to, frm = (y + dy) % NY, (y + NY - dy) % NY
        return device(z, xx, to), xx * NY + to, xx * NY + frm

    core_peer = device(z, xl, y, xh, 1 - core)
    high_peer = device(z, xl, y, 1 - xh, core)

    barrier = pltpu.get_barrier_semaphore()
    along_z = [peer("z", d)[0] for d in (1, NZ - 1)]
    along_y = [peer("y", d)[0] for d in (1, NY - 1)]
    partners = [core_peer, high_peer, peer("x", 1)[0]] + along_z + along_y
    for p in partners:
        pl.semaphore_signal(barrier, inc=1, device_id=p, device_id_type=MESH)
    rounds = (along_z + along_y, along_z + along_y, along_z)

    def tell(i):
        for p in rounds[i]:
            pl.semaphore_signal(ready.at[i], inc=1, device_id=p, device_id_type=MESH)

    def told(i):
        pl.semaphore_wait(ready.at[i], len(rounds[i]))

    loads = {}

    def load(name, src, dst):
        c = pltpu.make_async_copy(src, dst, lsem.at[len(loads)])
        c.start()
        loads[name] = c

    part = pl.ds(pl.multiple_of(tp * depth, depth), depth)
    load("a0", act.at[0], act_v.at[0])
    load("p0", proj.at[0, part], p_v.at[0])
    load("p1", proj.at[1, part], p_v.at[1])

    def load_rest():
        load("a1", act.at[1], act_v.at[1])
        load("p2", proj.at[2, part], p_v.at[2])
        for k in range(3):
            load(f"s{k}", sig.at[k], sig_v.at[k])
        own = pl.ds(pl.multiple_of(dp * rows, rows), rows)
        load("pl", proj.at[:, own], ploc_v)
        load("m1", first, m1_v)
        load("m2", second, m2_v)
        load("w", weights, w_v)


    sends = []

    def remote(src, dst, sem, to):
        return pltpu.make_async_remote_copy(
            src_ref=src, dst_ref=dst, send_sem=ssem.at[sem], recv_sem=rsem.at[sem],
            device_id=to, device_id_type=MESH,
        )

    def send(src, dst, sem, to):
        c = remote(src, dst, sem, to)
        c.start()
        sends.append(c)

    def send_all(copies, whole, sem):
        for src, dst, to in copies:
            remote(src, dst, sem, to).start()
        sends.append(remote(whole, whole, sem, copies[0][2]))

    counter = [0]

    def sems(n):
        counter[0] += n
        return counter[0] - n

    core_one, high_one, core_two = sems(3), sems(3), sems(3)

    def project(k):
        source = (0, 0, 1)[k]
        value = jnp.dot(act_v[source], p_v[k], preferred_element_type=F32)
        qp[k] = value.reshape(2, half, value.shape[1])

    perms = {route: permutation(route, 128) for route in {p[3]: 0 for p in PARTS}}
    base = [[sems(1) for g in p[3]] for p in PARTS]
    base_back = [[sems(1) for g in p[3]] for p in PARTS]

    def core_send(k):
        if k != 1:
            loads[("a0", "", "a1")[k]].wait()
        loads[f"p{k}"].wait()
        if k == 0:
            load_rest()
        project(k)
        if k == 0:
            pl.semaphore_wait(barrier, len(partners))
        send(qp.at[k, 1 - core], rc.at[k], core_one + k, core_peer)

    def high_send(k):
        remote(qp.at[k, 0], rc.at[k], core_one + k, core_peer).wait_recv()
        total = qp[k, core] + rc[k]
        rc[k] = total
        sx[k] = total.astype(BF16)
        send(sx.at[k], rx.at[k], high_one + k, high_peer)

    def core_back(k):
        remote(sx.at[k], rx.at[k], high_one + k, high_peer).wait_recv()
        q_v[k, core] = (rc[k] + rx[k].astype(F32)).astype(BF16)
        send(q_v.at[k, core], q_v.at[k, core], core_two + k, core_peer)

    def partners_of(p, stage):
        group = PARTS[p][3][stage]
        return [peer(group, d) for d in range(1, SIZES[group])]

    def scatter(p, stage, src, recv):
        copies = [(src.at[idx], recv.at[i], to) for i, (to, idx, _) in enumerate(partners_of(p, stage))]
        send_all(copies, src.at[pl.ds(0, len(copies))], base[p][stage])

    def arrived(p, stage, src, recv):
        to = partners_of(p, stage)[0][0]
        remote(recv, recv, base[p][stage], to).wait_recv()

    def gradient_of(k):
        remote(q_v.at[k, 1 - core], q_v.at[k, 1 - core], core_two + k, core_peer).wait_recv()
        q = q_v[k].reshape(tokens, 128)
        loads[f"s{k}"].wait()
        for p, part in enumerate(PARTS):
            if part[0] != k:
                continue
            turned = lax.dot_general(
                perms[part[3]], q, (((1,), (1,)), ((), ())), preferred_element_type=F32
            ).astype(BF16)
            start, size = part[1:3]
            lead = grads[p].shape[:-1]
            for at, w in blocks(size):
                value = lax.dot_general(
                    turned, sig_v[k, start + at : start + at + w, :], (((1,), (1,)), ((), ())),
                    preferred_element_type=F32,
                )
                grads[p][..., at : at + w] = value.astype(BF16).reshape(lead + (w,))
            scatter(p, 0, grads[p], firsts[p])

    def summed(src, recv, idx, at, w):
        total = src[idx, ..., at : at + w].astype(F32)
        for i in range(recv.shape[0]):
            total = total + recv[i, ..., at : at + w].astype(F32)
        return total

    def to_pieces(p, total, at, w):
        for i in range(8):
            sl[p][i, :, at : at + w] = total[2 * i : 2 * i + 2].astype(BF16)

    def first_sum(p):
        route = PARTS[p][3]
        arrived(p, 0, grads[p], firsts[p])
        for at, w in blocks(PARTS[p][2]):
            total = summed(grads[p], firsts[p], index[route[0]], at, w)
            if len(route) == 2:
                to_pieces(p, total, at, w)
            else:
                seconds[p][:, :, at : at + w] = total.astype(BF16)
        if len(route) == 2:
            scatter(p, 1, sl[p], rl[p])
        else:
            scatter(p, 1, seconds[p], second_recv[p])

    def second_sum(p):
        route = PARTS[p][3]
        if len(route) == 2:
            return
        arrived(p, 1, seconds[p], second_recv[p])
        for at, w in blocks(PARTS[p][2]):
            to_pieces(p, summed(seconds[p], second_recv[p], index[route[1]], at, w), at, w)
        scatter(p, 2, sl[p], rl[p])

    count = float(tokens * NZ * NX * NY)

    def update(p):
        k, _, _, route = PARTS[p]
        last = len(route) - 1
        arrived(p, last, sl[p], rl[p])
        idx = index[route[last]]
        start, size = PARTS[p][1:3]
        for at, w in blocks(size):
            cols = slice(start + at, start + at + w)
            gradient = summed(sl[p], rl[p], idx, at, w) / count
            one = beta_one * m1_v[k, :, cols] + (1.0 - beta_one) * gradient
            two = beta_two * m2_v[k, :, cols] + (1.0 - beta_two) * gradient * gradient
            heading = one / first_fix / (jnp.sqrt(two / second_fix) + adam_eps)
            new_first[k, :, cols] = one
            new_second[k, :, cols] = two
            new_dir[k, :, cols] = heading
            gl[p][idx, :, at : at + w] = heading.astype(BF16)
        copies = [(gl[p].at[idx], gl[p].at[idx], to) for to, _, _ in partners_of(p, last)]
        send_all(copies, gl[p].at[pl.ds(0, 7)], base_back[p][last])

    def place(p, stage):
        return tuple(index[g] for g in PARTS[p][3][: stage + 1])

    def others(p, stage):
        lead = place(p, stage)[:-1]
        return dirs[p].at[lead + (pl.ds(0, SIZES[PARTS[p][3][stage]] - 1),)]

    def spread(p, stage):
        slot = dirs[p].at[place(p, stage)]
        copies = [(slot, slot, to) for to, _, _ in partners_of(p, stage)]
        send_all(copies, others(p, stage), base_back[p][stage])

    def gathered(p, stage):
        to = partners_of(p, stage)[0][0]
        remote(others(p, stage), others(p, stage), base_back[p][stage], to).wait_recv()

    def joined(p):
        route = PARTS[p][3]
        last = len(route) - 1
        seven = gl[p].at[pl.ds(0, 7)]
        remote(seven, seven, base_back[p][last], partners_of(p, last)[0][0]).wait_recv()
        at16 = place(p, last - 1)
        for at, w in blocks(PARTS[p][2]):
            pieces = [gl[p][i, :, at : at + w].astype(F32) for i in range(8)]
            dirs[p][at16 + (slice(None), slice(at, at + w))] = jnp.concatenate(pieces, axis=0).astype(BF16)
        spread(p, last - 1)

    def middle(p):
        if len(PARTS[p][3]) == 3:
            gathered(p, 1)
            spread(p, 0)

    def finish(p):
        k, _, _, route = PARTS[p]
        gathered(p, 0)
        basis = lax.dot_general(
            ploc_v[k], perms[route], (((1,), (1,)), ((), ())), preferred_element_type=F32
        ).astype(BF16)
        start, size = PARTS[p][1:3]
        for at, w in blocks(size):
            cols = slice(start + at, start + at + w)
            heading = dirs[p][..., at : at + w].reshape(128, w)
            change = jnp.dot(basis, heading, preferred_element_type=F32)
            new_weights[k, :, cols] = (w_v[k, :, cols].astype(F32) - learning_rate * change).astype(BF16)

    core_send(0)
    tell(0)
    core_send(1)
    high_send(0)
    told(0)
    tell(1)
    core_send(2)
    high_send(1)
    high_send(2)
    told(1)
    tell(2)
    core_back(0)
    core_back(1)
    told(2)
    gradient_of(0)
    core_back(2)
    gradient_of(1)
    gradient_of(2)

    for name in ("m1", "m2", "pl", "w"):
        loads[name].wait()
    for op, p in (
        (first_sum, 1), (first_sum, 0), (first_sum, 2), (first_sum, 4), (first_sum, 5), (second_sum, 1),
        (second_sum, 0), (second_sum, 2), (second_sum, 5), (first_sum, 3), (second_sum, 4), (update, 1),
        (update, 0), (update, 2), (update, 3), (update, 5), (update, 4), (joined, 0),
        (joined, 3), (joined, 1), (joined, 2), (joined, 5), (joined, 4), (middle, 1),
        (middle, 0), (middle, 2), (middle, 5), (middle, 4), (finish, 0), (finish, 2),
        (finish, 1), (finish, 3), (finish, 4), (finish, 5),
    ):
        op(p)
    for c in sends:
        c.wait_send()


def write_out(*refs):
    sem = refs[8]
    copies = [pltpu.make_async_copy(refs[0].at[k], refs[4].at[k], sem.at[3 + k]) for k in range(3)]
    copies += [pltpu.make_async_copy(refs[i], refs[4 + i], sem.at[i - 1]) for i in range(1, 4)]
    for c in copies:
        c.start()
    for c in copies:
        c.wait()


def on_device(activations, signals, projectors, weights, first_moment, second_moment):
    signals = jnp.transpose(signals, (0, 2, 1))
    _, tokens, depth = activations.shape
    _, width, _ = signals.shape
    rank = projectors.shape[2]
    rows = weights.shape[1]
    half = tokens // 2
    small = first_moment.shape
    vmem = pltpu.VMEM
    lead = [route_rows(p[3]) for p in PARTS]
    cells = [(16, p[2]) for p in PARTS]

    def small_like(n):
        return [vmem((n, 2, c[1]), BF16) for c in cells]

    scratch = [
        vmem(activations.shape, BF16), vmem(signals.shape, BF16), vmem((3, depth, rank), BF16),
        vmem((3, rows, rank), BF16), vmem(weights.shape, BF16), vmem(small, F32), vmem(small, F32),
        vmem((3, 2, half, rank), F32), vmem((3, half, rank), F32), vmem((3, half, rank), BF16),
        vmem((3, half, rank), BF16), vmem((3, 2, half, rank), BF16),
    ]
    scratch += [vmem(l + c, BF16) for l, c in zip(lead, cells)]
    scratch += [vmem((l[0] - 1,) + l[1:] + c, BF16) for l, c in zip(lead, cells)]
    scratch += [vmem((l + (1,))[1:2] + c, BF16) for l, c in zip(lead, cells)]
    scratch += [vmem((max((l + (1,))[1] - 1, 1),) + c, BF16) for l, c in zip(lead, cells)]
    scratch += small_like(8) + small_like(7) + small_like(8)
    scratch += [vmem(l + c, BF16) for l, c in zip(lead, cells)]
    n_sem = 9 + 2 * sum(len(p[3]) for p in PARTS)
    scratch += [
        pltpu.SemaphoreType.DMA((12,)), pltpu.SemaphoreType.DMA((n_sem,)), pltpu.SemaphoreType.DMA((n_sem,)),
        pltpu.SemaphoreType.REGULAR((3,)),
    ]
    results = ((weights.shape, BF16), (small, F32), (small, F32), (small, F32))
    held = pl.pallas_call(
        kernel,
        out_shape=tuple(vmem(*r) for r in results),
        in_specs=[pl.BlockSpec(memory_space=pltpu.HBM)] * 6,
        out_specs=(pl.BlockSpec(memory_space=vmem),) * 4,
        scratch_shapes=scratch,
        compiler_params=pltpu.CompilerParams(
            collective_id=0, has_side_effects=True, vmem_limit_bytes=60 << 20
        ),
        name="lowrank_adam",
    )(activations, signals, projectors, weights, first_moment, second_moment)
    held = [pltpu.with_memory_space_constraint(h, vmem) for h in held]
    return pl.pallas_call(
        write_out,
        out_shape=tuple(jax.ShapeDtypeStruct(*r) for r in results),
        in_specs=[pl.BlockSpec(memory_space=vmem)] * 4,
        out_specs=(pl.BlockSpec(memory_space=pltpu.HBM),) * 4,
        scratch_shapes=[pltpu.SemaphoreType.DMA((6,))],
        name="write_out",
    )(*held)


def solution(mesh):
    split = P(None, "dp", "tensor")
    return jax.shard_map(
        on_device,
        mesh=mesh,
        in_specs=(split, split, P(), split, split, split),
        out_specs=(split, split, split, split),
        check_vma=False,
    )
```
